32 devices in a mesh: grp: 16 (over z, y, x), dir: 2 (over core).
Axes of the slice: x: 2, y: 2, z: 4, core: 2. Of those that a mesh axis runs over, the one named last changes fastest.
Arguments:
- currents_hist: bfloat16 [6, 64, 256], P(None, 'grp'), may hold values from -6 to 6
- spectra_hist: bfloat16 [64, 64, 512], P(None, 'grp', 'dir'), may hold values from -6 to 6
- excitation: float32 [2, 64, 256], P(None, 'grp'), may hold values from -6 to 6
- near_blocks: bfloat16 [64, 8, 6, 256, 256], P('grp', 'dir'), may hold values from -0.0546875 to 0.0546875
- self_inverse: float32 [64, 256, 256], P('grp'), may hold values from -0.375 to 0.375
- aggregate: bfloat16 [64, 256, 512], P('grp', None, 'dir'), may hold values from -0.375 to 0.375
- translate: float32 [64, 512], P(None, 'dir'), may hold values from -1.5 to 1.5
- neighbours: int32 [64, 8], P('grp', 'dir'), may hold values from 0 to 63, as said below
- counts: int32 [64], P('grp'), may hold values from 1 to 8, as said below
- far_sources: int32 [64, 16], P('grp'), may hold values from 0 to 63
- far_classes: int32 [64, 16], P('grp'), may hold values from 0 to 63
- delays: int32 [64], replicated, may hold values from 1 to 64
Outputs:
- currents: bfloat16 [2, 64, 256], P(None, 'grp')
- spectra: bfloat16 [2, 64, 512], P(None, 'grp', 'dir')
The draws below stay inside these ranges and needn't reach their ends.
Inputs may be any that keep to these rules, and one draw needn't show every extreme that they name: neighbours[g, 0] = g; every neighbour of group g lies among the groups of g's owner, g // 4, or of the owners one before and one after, at 4 groups an owner. `counts`: the first group has all slots live and the last group one.
All inputs are finite; a program needn't handle non-finite values.
Results may differ from the reference program's by a relative error of at most 0.0095.
Values may be sent and summed in bfloat16 or wider, within the bound.
A program may use at most 64 MiB of HBM per device.

```python
import jax
import jax.numpy as jnp
from jax import lax

NB = 256
G_DEV = 4
K = 8
LAGS = 6
HF = 64
F = 16
NCLS = 64
DIRS = 512
STEPS = 2
G = 64


def draw_neighbours(key, part):
    groups = jnp.arange(G, dtype=jnp.int32)
    owners = groups // G_DEV
    lowest = jnp.maximum(owners - 1, 0) * G_DEV
    highest = jnp.minimum(owners + 2, G // G_DEV) * G_DEV
    window_size = highest - lowest
    drawn = jax.random.randint(key, (G, K), 0, 1 << 20, dtype=jnp.int32)
    result = lowest[:, None] + drawn % window_size[:, None]
    return result.at[:, 0].set(groups)


def draw_counts(key, part):
    drawn = jax.random.randint(key, (G,), 1, K + 1, dtype=jnp.int32)
    return drawn.at[0].set(K).at[G - 1].set(1)


def draw_far_sources(key, part):
    drawn = jax.random.randint(key, (G, F), 0, G, dtype=jnp.int32)
    return drawn.at[0, 0].set(G - 1).at[G - 1, 0].set(0)


def draw_far_classes(key, part):
    drawn = jax.random.randint(key, (G, F), 0, NCLS, dtype=jnp.int32)
    return drawn.at[0, 0].set(NCLS - 1).at[G - 1, 0].set(0)


def draw_delays(key, part):
    cycle = jnp.arange(NCLS, dtype=jnp.int32) % HF
    return jax.random.permutation(key, cycle) + 1


def levels(stream_key, shape, split, smallest, top_value):
    level = 1.0
    for dim, blocks in split:
        heights = jax.random.uniform(jax.random.fold_in(jax.random.fold_in(stream_key, 6), dim), (blocks,), jnp.float32, smallest / len(split), top_value / len(split))
        level = level * jnp.repeat(jnp.exp(heights), shape[dim] // blocks).reshape((-1,) + (1,) * (len(shape) - 1 - dim))
    return level


def scatter_about(key, shape, width, most, cuts=(), kind=jnp.bfloat16):
    values = jax.random.normal(key, shape, jnp.float32) * width
    if len(cuts) > 0:
        values = levels(key, shape, cuts, -0.22, 0.18) * values
    return jnp.clip(values, min=-most, max=most).astype(kind)


def setup_inputs(seed: int = 0) -> dict:
    seeds = jax.random.split(jax.random.key(seed), 13)
    return {
        "currents_hist": scatter_about(seeds[0], (LAGS, G, NB), 1.0, 6.0, ((1, 16),)),
        "spectra_hist": scatter_about(seeds[1], (HF, G, DIRS), 1.0, 6.0, ((1, 16), (2, 2))),
        "excitation": scatter_about(seeds[2], (STEPS, G, NB), 1.0, 6.0, ((1, 16),), jnp.float32),
        "near_blocks": scatter_about(seeds[3], (G, K, LAGS, NB, NB), (NB * K * LAGS) ** -0.5, 0.0546875, ((0, 16), (1, 2))),
        "self_inverse": scatter_about(seeds[4], (G, NB, NB), NB ** -0.5, 0.375, ((0, 16),), jnp.float32),
        "aggregate": scatter_about(seeds[5], (G, NB, DIRS), NB ** -0.5, 0.375, ((0, 16), (2, 2))),
        "translate": scatter_about(seeds[6], (NCLS, DIRS), F ** -0.5, 1.5, ((1, 2),), jnp.float32),
        "neighbours": draw_neighbours(jax.random.fold_in(seeds[12], 71), 0),
        "counts": draw_counts(jax.random.fold_in(seeds[12], 71), 0),
        "far_sources": draw_far_sources(jax.random.fold_in(seeds[12], 71), 0),
        "far_classes": draw_far_classes(jax.random.fold_in(seeds[12], 71), 0),
        "delays": draw_delays(jax.random.fold_in(seeds[12], 71), 0),
    }


def reference(currents_hist, spectra_hist, excitation, near_blocks, self_inverse, aggregate, translate, neighbours, counts, far_sources, far_classes, delays):
    slot_ids = jnp.arange(K, dtype=jnp.int32)
    slot_mask = (slot_ids[None, :] < counts[:, None]).astype(jnp.float32)
    lag_index = delays[far_classes] - 1
    factors = translate[far_classes]
    agg_wide = aggregate.astype(jnp.float32)

    def near_field(history):
        def group_near(operands):
            blocks, neighbour_ids, live_row = operands
            selected = history[:, neighbour_ids, :].astype(jnp.float32) * live_row[None, :, None]
            return jnp.einsum("klrc,lkc->r", blocks.astype(jnp.float32), selected)
        return lax.map(group_near, (near_blocks, neighbours, slot_mask))

    def far_field(spectra_now):
        values = spectra_now[lag_index, far_sources, :].astype(jnp.float32)
        incoming = jnp.sum(values * factors, axis=1).astype(jnp.bfloat16)
        return jnp.einsum("gbd,gd->gb", agg_wide, incoming.astype(jnp.float32))

    currents_now = currents_hist
    spectra_now = spectra_hist
    out_currents = []
    out_spectra = []
    for iteration in range(STEPS):
        summed = near_field(currents_now) + far_field(spectra_now)
        remainder = excitation[iteration] - summed
        solved = jnp.einsum("grc,gc->gr", self_inverse, remainder, precision=lax.Precision.HIGHEST)
        stored = solved.astype(jnp.bfloat16)
        spectrum = jnp.einsum("gbd,gb->gd", agg_wide, stored.astype(jnp.float32)).astype(jnp.bfloat16)
        currents_now = jnp.concatenate([stored[None], currents_now[:-1]], axis=0)
        spectra_now = jnp.concatenate([spectrum[None], spectra_now[:-1]], axis=0)
        out_currents.append(stored)
        out_spectra.append(spectrum)
    return jnp.stack(out_currents), jnp.stack(out_spectra)
```

```python
import functools

import jax
import jax.numpy as jnp
from jax import lax
from jax.experimental import pallas as pl
from jax.experimental.pallas import tpu as pltpu
from jax.sharding import PartitionSpec as P

STEPS = 2
MESH = pl.DeviceIdType.MESH
F32 = jnp.float32
BF16 = jnp.bfloat16


def mm(a, b, ca=1, cb=0):
    return lax.dot_general(a, b, (((ca,), (cb,)), ((), ())), preferred_element_type=F32)


def parts(x):
    high = x.astype(BF16)
    return high, (x - high.astype(F32)).astype(BF16)


def kernel(
    n,
    nd,
    nbr_s,
    cnt_s,
    hist_v,
    spec_v,
    exc_v,
    src_v,
    cls_v,
    del_v,
    tr_v,
    near_h,
    inv_h,
    agg_h,
    cur_o,
    spec_o,
    near_v,
    inv_v,
    agg_v,
    inv_hi,
    inv_lo,
    codes,
    win,
    cwin,
    nacc,
    out1,
    out2,
    in1,
    in2,
    sums,
    wide,
    near_sem,
    inv_sem,
    agg_sem,
    code_tx,
    code_rx,
    win_tx,
    win_rx,
    cwin_tx,
    cwin_rx,
    p1_tx,
    p1_rx,
    p2_tx,
    p2_rx,
    sum_tx,
    sum_rx,
):
    gd, slots, lags, nb, _ = near_h.shape
    hf, _, dirs = spec_v.shape
    ncls = tr_v.shape[0]
    far = src_v.shape[1]
    packed = in1.shape[2] != dirs
    me = lax.axis_index("grp")
    mine = lax.axis_index("dir")
    following, before = lax.rem(me + 1, n), lax.rem(me + n - 1, n)

    def near_copy(i):
        g, k = i // slots, i % slots
        return pltpu.make_async_copy(near_h.at[g, k], near_v.at[g, k], near_sem.at[i])

    agg_copy = pltpu.make_async_copy(agg_h, agg_v, agg_sem)
    inv_copy = pltpu.make_async_copy(inv_h, inv_v, inv_sem)

    barrier = pltpu.get_barrier_semaphore()

    @pl.loop(1, n)
    def _(off):
        pl.semaphore_signal(barrier, inc=1, device_id={"grp": lax.rem(me + off, n)}, device_id_type=MESH)

    for off in range(1, nd):
        pl.semaphore_signal(barrier, inc=1, device_id={"dir": lax.rem(mine + off, nd)}, device_id_type=MESH)

    inv_copy.start()

    @pl.loop(0, gd * slots)
    def _(i):
        near_copy(i).start()

    agg_copy.start()

    own = src_v[...] * ncls + cls_v[...]
    codes[me] = jnp.full(codes.shape[1:], -1, jnp.int32)
    codes[me, 0:gd, 0:far] = own
    codes[me, gd : 2 * gd, 0:far] = own
    win[pl.ds(gd, gd)] = jnp.zeros((gd,) + win.shape[1:], F32)
    for lag in range(lags):
        row = hist_v[lag].astype(F32)
        for g in range(gd):
            win[gd + g, lag : lag + 1, :] = row[g : g + 1, :]

    pl.semaphore_wait(barrier, n - 1 + nd - 1)

    def send_all(src, dst, tx, rx):
        def copy(peer, slot):
            return pltpu.make_async_remote_copy(
                src_ref=src(peer),
                dst_ref=dst.at[slot],
                send_sem=tx.at[peer],
                recv_sem=rx.at[slot],
                device_id={"grp": peer},
                device_id_type=MESH,
            )

        @pl.loop(1, n)
        def _(off):
            copy(lax.rem(me + off, n), me).start()

        def arrive():
            @pl.loop(1, n)
            def _(off):
                peer = lax.rem(me + off, n)
                copy(peer, peer).wait_recv()

        def sent():
            @pl.loop(1, n)
            def _(off):
                copy(lax.rem(me + off, n), me).wait_send()

        return arrive, sent

    def send_sides(ref, tx, rx):
        def copy(i, peer, start):
            return pltpu.make_async_remote_copy(
                src_ref=ref.at[pl.ds(gd, gd)],
                dst_ref=ref.at[pl.ds(start, gd)],
                send_sem=tx.at[i],
                recv_sem=rx.at[i],
                device_id={"grp": peer},
                device_id_type=MESH,
            )

        both = (copy(0, following, 0), copy(1, before, 2 * gd))
        for c in both:
            c.start()
        return both

    codes_in, codes_out = send_all(lambda peer: codes.at[me], codes, code_tx, code_rx)
    sides = send_sides(win, win_tx, win_rx)

    lag_ids = lax.broadcasted_iota(jnp.int32, (hf, ncls), 0)
    delay = del_v[...]
    pick1 = (lag_ids == delay - 1).astype(F32).T.astype(BF16)
    pick2 = (lag_ids == delay - 2).astype(F32).T.astype(BF16)
    pick = jnp.concatenate([pick1, pick2], axis=0)
    newest = (lax.broadcasted_iota(jnp.int32, (hf, dirs), 0) == 0).astype(BF16)
    factor = tr_v[...]
    fresh = factor * mm(pick1, newest)
    wide[...] = spec_v[...].astype(F32)
    first, second = [], []
    for s in range(gd):
        got = mm(pick, wide[:, s, :].astype(BF16))
        first.append(factor * got[0:ncls])
        second.append(factor * got[ncls : 2 * ncls])
    p1 = parts(jnp.concatenate(first, axis=0))
    p2 = parts(jnp.concatenate(second, axis=0))

    inv_copy.wait()
    for g in range(gd):
        high, low = parts(inv_v[g])
        inv_hi[g] = high
        inv_lo[g] = low

    def pack(x):
        x = x.reshape(n, 2 * gd, dirs)
        if not packed:
            return x
        half = dirs // 2
        rows = lax.broadcasted_iota(jnp.int32, (n, 2 * gd, half), 1)
        return jnp.where(rows < gd, x[:, :, :half], x[:, :, half:])

    def unpack(x):
        if not packed:
            return x
        low = jnp.concatenate([x[0:gd], x[0:gd]], axis=0)
        high = jnp.concatenate([x[gd:], x[gd:]], axis=0)
        return jnp.concatenate([low, high], axis=1)

    codes_in()
    key = codes[...].reshape(n * 2 * gd, codes.shape[2]) - me * (gd * ncls)
    ids = lax.broadcasted_iota(jnp.int32, (n * 2 * gd, gd * ncls), 1)
    weight = jnp.zeros(ids.shape, F32)
    for f in range(far):
        weight += (key[:, f : f + 1] == ids).astype(F32)
    weight = weight.astype(BF16)
    out1[...] = pack(mm(weight, p1[0]) + mm(weight, p1[1]))
    in1[me] = out1[me]
    p1_in, p1_out = send_all(lambda peer: out1.at[peer], in1, p1_tx, p1_rx)
    older = mm(weight, p2[0]) + mm(weight, p2[1])

    for c in sides:
        c.wait_recv()

    @pl.loop(0, gd)
    def _(g):
        acc = [jnp.zeros((8, nb), F32)] * lags
        for k in range(slots):
            near_copy(g * slots + k).wait()
            local = jnp.clip(nbr_s[g, k] - (me - 1) * gd, 0, 3 * gd - 1)
            alive = (mine * slots + k < cnt_s[g]).astype(F32)
            row = (win[local] * alive).astype(BF16)
            for lag in range(lags):
                acc[lag] += mm(row, near_v[g, k, lag], 1, 1)
        now = acc[0][0:1]
        later = jnp.zeros((1, nb), F32)
        for lag in range(1, lags):
            now += acc[lag][lag : lag + 1]
            later += acc[lag][lag - 1 : lag]
        nacc[g, 0:1, :] = now
        nacc[g, 1:2, :] = later

    agg_copy.wait()

    def solve(step, near, incoming):
        inc = incoming.astype(BF16)
        rows = [near[g] + mm(inc, agg_v[g], 1, 1)[g : g + 1] for g in range(gd)]
        sums[step, mine] = jnp.concatenate(rows, axis=0)

        def copy(peer, slot):
            return pltpu.make_async_remote_copy(
                src_ref=sums.at[step, mine],
                dst_ref=sums.at[step, slot],
                send_sem=sum_tx.at[step, peer],
                recv_sem=sum_rx.at[step, slot],
                device_id={"dir": peer},
                device_id_type=MESH,
            )

        for off in range(1, nd):
            copy(lax.rem(mine + off, nd), mine).start()
        for off in range(1, nd):
            peer = lax.rem(mine + off, nd)
            copy(peer, peer).wait_recv()
        total = sums[step, 0]
        for d in range(1, nd):
            total += sums[step, d]
        rest = exc_v[step] - total
        rest = jnp.concatenate([rest, rest], axis=0)
        high, low = parts(rest)
        both = jnp.concatenate([high, low], axis=0)
        rows = []
        for g in range(gd):
            a = mm(both, inv_hi[g], 1, 1)
            b = mm(high, inv_lo[g], 1, 1)
            rows.append(a[g : g + 1] + a[2 * gd + g : 2 * gd + g + 1] + b[g : g + 1])
        for off in range(1, nd):
            copy(lax.rem(mine + off, nd), mine).wait_send()
        stored = jnp.concatenate(rows, axis=0).astype(BF16)
        cur_o[step] = stored
        return stored

    def radiate(step, stored):
        twice = jnp.concatenate([stored.astype(F32)] * 2, axis=0).astype(BF16)
        rows = [mm(twice, agg_v[g])[g : g + 1] for g in range(gd)]
        spectrum = jnp.concatenate(rows, axis=0).astype(BF16)
        spec_o[step] = spectrum
        return spectrum

    p1_in()
    stored = solve(0, [nacc[g, 0:1, :] for g in range(gd)], unpack(jnp.sum(in1[...], axis=0)))
    wider = stored.astype(F32)
    for g in range(gd):
        cwin[gd + g] = wider[g : g + 1]
    cur_sides = send_sides(cwin, cwin_tx, cwin_rx)
    spectrum = radiate(0, stored).astype(F32)
    q = parts(jnp.concatenate([fresh * spectrum[s : s + 1] for s in range(gd)], axis=0))
    out2[...] = pack(older + mm(weight, q[0]) + mm(weight, q[1]))
    in2[me] = out2[me]
    p2_in, p2_out = send_all(lambda peer: out2.at[peer], in2, p2_tx, p2_rx)
    for c in cur_sides:
        c.wait_recv()
    near = []
    for g in range(gd):
        total = nacc[g, 1:2, :]
        for k in range(slots):
            local = jnp.clip(nbr_s[g, k] - (me - 1) * gd, 0, 3 * gd - 1)
            alive = (mine * slots + k < cnt_s[g]).astype(F32)
            row = (cwin[local] * alive).astype(BF16)
            total += mm(row, near_v[g, k, 0], 1, 1)
        near.append(total)
    p2_in()
    stored = solve(1, near, unpack(jnp.sum(in2[...], axis=0)))
    radiate(1, stored)
    for c in sides:
        c.wait_send()
    for c in cur_sides:
        c.wait_send()
    codes_out()
    p1_out()
    p2_out()


def per_device(
    currents_hist,
    spectra_hist,
    excitation,
    near_blocks,
    self_inverse,
    aggregate,
    translate,
    neighbours,
    counts,
    far_sources,
    far_classes,
    delays,
):
    n, nd = lax.axis_size("grp"), lax.axis_size("dir")
    gd, slots, lags, nb, _ = near_blocks.shape
    hf, _, dirs = spectra_hist.shape
    lane = dirs // 2 if dirs % 256 == 0 else dirs
    vmem = pl.BlockSpec(memory_space=pltpu.VMEM)
    smem = pl.BlockSpec(memory_space=pltpu.SMEM)
    anywhere = pl.BlockSpec(memory_space=pl.ANY)
    dma = pltpu.SemaphoreType.DMA
    return pl.pallas_call(
        functools.partial(kernel, n, nd),
        out_shape=(
            jax.ShapeDtypeStruct((STEPS, gd, nb), BF16),
            jax.ShapeDtypeStruct((STEPS, gd, dirs), BF16),
        ),
        in_specs=[smem] * 2 + [vmem] * 7 + [anywhere] * 3,
        out_specs=(vmem, vmem),
        scratch_shapes=[
            pltpu.VMEM(near_blocks.shape, BF16),
            pltpu.VMEM(self_inverse.shape, F32),
            pltpu.VMEM(aggregate.shape, BF16),
            pltpu.VMEM(self_inverse.shape, BF16),
            pltpu.VMEM(self_inverse.shape, BF16),
            pltpu.VMEM((n, 2 * gd, 128), jnp.int32),
            pltpu.VMEM((3 * gd, 8, nb), F32),
            pltpu.VMEM((3 * gd, 1, nb), F32),
            pltpu.VMEM((gd, 8, nb), F32),
            pltpu.VMEM((n, 2 * gd, lane), F32),
            pltpu.VMEM((n, 2 * gd, lane), F32),
            pltpu.VMEM((n, 2 * gd, lane), F32),
            pltpu.VMEM((n, 2 * gd, lane), F32),
            pltpu.VMEM((STEPS, nd, gd, nb), F32),
            pltpu.VMEM((hf, gd, dirs), F32),
            dma((gd * slots,)),
            dma,
            dma,
            dma((n,)),
            dma((n,)),
            dma((2,)),
            dma((2,)),
            dma((2,)),
            dma((2,)),
            dma((n,)),
            dma((n,)),
            dma((n,)),
            dma((n,)),
            dma((STEPS, nd)),
            dma((STEPS, nd)),
        ],
        compiler_params=pltpu.CompilerParams(
            collective_id=0, has_side_effects=True, vmem_limit_bytes=48 * 1024 * 1024
        ),
        name="march",
    )(
        neighbours,
        counts,
        currents_hist,
        spectra_hist,
        excitation,
        far_sources,
        far_classes,
        delays.reshape(1, -1),
        translate,
        near_blocks,
        self_inverse,
        aggregate,
    )


def solution(mesh):
    placed = (
        P(None, "grp", None),
        P(None, "grp", "dir"),
        P(None, "grp", None),
        P("grp", "dir", None, None, None),
        P("grp", None, None),
        P("grp", None, "dir"),
        P(None, "dir"),
        P("grp", "dir"),
        P("grp"),
        P("grp", None),
        P("grp", None),
        P(),
    )
    return jax.shard_map(
        per_device,
        mesh=mesh,
        in_specs=placed,
        out_specs=(P(None, "grp", None), P(None, "grp", "dir")),
        check_vma=False,
    )
```

```python
import functools

import jax
import jax.numpy as jnp
from jax import lax
from jax.experimental import pallas as pl
from jax.experimental.pallas import tpu as pltpu
from jax.sharding import PartitionSpec as P

STEPS = 2
MESH = pl.DeviceIdType.MESH
F32 = jnp.float32
BF16 = jnp.bfloat16


def mm(a, b, ca=1, cb=0):
    return lax.dot_general(a, b, (((ca,), (cb,)), ((), ())), preferred_element_type=F32)


def parts(x):
    high = x.astype(BF16)
    return high, (x - high.astype(F32)).astype(BF16)


def kernel(
    n,
    nd,
    nbr_h,
    cnt_h,
    hist_h,
    spec_h,
    exc_h,
    src_h,
    cls_h,
    del_h,
    tr_h,
    near_h,
    inv_h,
    agg_h,
    cur_o,
    spec_o,
    nbr_s,
    cnt_s,
    hist_v,
    spec_v,
    exc_v,
    src_v,
    cls_v,
    del_v,
    tr_v,
    small_sem,
    near_v,
    inv_v,
    agg_v,
    inv_hi,
    inv_lo,
    codes,
    win,
    cwin,
    nacc,
    out1,
    out2,
    in1,
    in2,
    sums,
    wide,
    near_sem,
    inv_sem,
    agg_sem,
    code_tx,
    code_rx,
    win_tx,
    win_rx,
    cwin_tx,
    cwin_rx,
    p1_tx,
    p1_rx,
    p2_tx,
    p2_rx,
    sum_tx,
    sum_rx,
):
    gd, slots, lags, nb, _ = near_h.shape
    hf, _, dirs = spec_v.shape
    ncls = tr_v.shape[0]
    far = src_v.shape[1]
    packed = in1.shape[2] != dirs
    me = lax.axis_index("grp")
    mine = lax.axis_index("dir")
    following, before = lax.rem(me + 1, n), lax.rem(me + n - 1, n)

    def near_copy(i):
        g, k = i // slots, i % slots
        return pltpu.make_async_copy(near_h.at[g, k], near_v.at[g, k], near_sem.at[i])

    smalls = (
        (src_h, src_v),
        (cls_h, cls_v),
        (hist_h, hist_v),
        (del_h, del_v),
        (spec_h, spec_v),
        (tr_h, tr_v),
        (nbr_h, nbr_s),
        (cnt_h, cnt_s),
        (exc_h, exc_v),
    )
    small_copies = [
        pltpu.make_async_copy(src, dst, small_sem.at[i]) for i, (src, dst) in enumerate(smalls)
    ]
    agg_copy = pltpu.make_async_copy(agg_h, agg_v, agg_sem)
    inv_copy = pltpu.make_async_copy(inv_h, inv_v, inv_sem)

    for c in small_copies:
        c.start()
    barrier = pltpu.get_barrier_semaphore()

    @pl.loop(1, n)
    def _(off):
        pl.semaphore_signal(barrier, inc=1, device_id={"grp": lax.rem(me + off, n)}, device_id_type=MESH)

    for off in range(1, nd):
        pl.semaphore_signal(barrier, inc=1, device_id={"dir": lax.rem(mine + off, nd)}, device_id_type=MESH)

    inv_copy.start()

    @pl.loop(0, gd * slots)
    def _(i):
        near_copy(i).start()

    agg_copy.start()

    for c in small_copies:
        c.wait()
    own = src_v[...] * ncls + cls_v[...]
    codes[me] = jnp.full(codes.shape[1:], -1, jnp.int32)
    codes[me, 0:gd, 0:far] = own
    codes[me, gd : 2 * gd, 0:far] = own
    win[pl.ds(gd, gd)] = jnp.zeros((gd,) + win.shape[1:], F32)
    for lag in range(lags):
        row = hist_v[lag].astype(F32)
        for g in range(gd):
            win[gd + g, lag : lag + 1, :] = row[g : g + 1, :]

    pl.semaphore_wait(barrier, n - 1 + nd - 1)

    def send_all(src, dst, tx, rx):
        def copy(peer, slot):
            return pltpu.make_async_remote_copy(
                src_ref=src(peer),
                dst_ref=dst.at[slot],
                send_sem=tx.at[peer],
                recv_sem=rx.at[slot],
                device_id={"grp": peer},
                device_id_type=MESH,
            )

        @pl.loop(1, n)
        def _(off):
            copy(lax.rem(me + off, n), me).start()

        def arrive():
            @pl.loop(1, n)
            def _(off):
                peer = lax.rem(me + off, n)
                copy(peer, peer).wait_recv()

        def sent():
            @pl.loop(1, n)
            def _(off):
                copy(lax.rem(me + off, n), me).wait_send()

        return arrive, sent

    def send_sides(ref, tx, rx):
        def copy(i, peer, start):
            return pltpu.make_async_remote_copy(
                src_ref=ref.at[pl.ds(gd, gd)],
                dst_ref=ref.at[pl.ds(start, gd)],
                send_sem=tx.at[i],
                recv_sem=rx.at[i],
                device_id={"grp": peer},
                device_id_type=MESH,
            )

        both = (copy(0, following, 0), copy(1, before, 2 * gd))
        for c in both:
            c.start()
        return both

    codes_in, codes_out = send_all(lambda peer: codes.at[me], codes, code_tx, code_rx)
    sides = send_sides(win, win_tx, win_rx)

    lag_ids = lax.broadcasted_iota(jnp.int32, (hf, ncls), 0)
    delay = del_v[...]
    pick1 = (lag_ids == delay - 1).astype(F32).T.astype(BF16)
    pick2 = (lag_ids == delay - 2).astype(F32).T.astype(BF16)
    pick = jnp.concatenate([pick1, pick2], axis=0)
    newest = (lax.broadcasted_iota(jnp.int32, (hf, dirs), 0) == 0).astype(BF16)
    factor = tr_v[...]
    fresh = factor * mm(pick1, newest)
    wide[...] = spec_v[...].astype(F32)
    first, second = [], []
    for s in range(gd):
        got = mm(pick, wide[:, s, :].astype(BF16))
        first.append(factor * got[0:ncls])
        second.append(factor * got[ncls : 2 * ncls])
    p1 = parts(jnp.concatenate(first, axis=0))
    p2 = parts(jnp.concatenate(second, axis=0))

    inv_copy.wait()
    for g in range(gd):
        high, low = parts(inv_v[g])
        inv_hi[g] = high
        inv_lo[g] = low

    def pack(x):
        x = x.reshape(n, 2 * gd, dirs)
        if not packed:
            return x
        half = dirs // 2
        rows = lax.broadcasted_iota(jnp.int32, (n, 2 * gd, half), 1)
        return jnp.where(rows < gd, x[:, :, :half], x[:, :, half:])

    def unpack(x):
        if not packed:
            return x
        low = jnp.concatenate([x[0:gd], x[0:gd]], axis=0)
        high = jnp.concatenate([x[gd:], x[gd:]], axis=0)
        return jnp.concatenate([low, high], axis=1)

    codes_in()
    key = codes[...].reshape(n * 2 * gd, codes.shape[2]) - me * (gd * ncls)
    ids = lax.broadcasted_iota(jnp.int32, (n * 2 * gd, gd * ncls), 1)
    weight = jnp.zeros(ids.shape, F32)
    for f in range(far):
        weight += (key[:, f : f + 1] == ids).astype(F32)
    weight = weight.astype(BF16)
    out1[...] = pack(mm(weight, p1[0]) + mm(weight, p1[1]))
    in1[me] = out1[me]
    p1_in, p1_out = send_all(lambda peer: out1.at[peer], in1, p1_tx, p1_rx)
    older = mm(weight, p2[0]) + mm(weight, p2[1])

    for c in sides:
        c.wait_recv()

    @pl.loop(0, gd)
    def _(g):
        acc = [jnp.zeros((8, nb), F32)] * lags
        for k in range(slots):
            near_copy(g * slots + k).wait()
            local = jnp.clip(nbr_s[g, k] - (me - 1) * gd, 0, 3 * gd - 1)
            alive = (mine * slots + k < cnt_s[g]).astype(F32)
            row = (win[local] * alive).astype(BF16)
            for lag in range(lags):
                acc[lag] += mm(row, near_v[g, k, lag], 1, 1)
        now = acc[0][0:1]
        later = jnp.zeros((1, nb), F32)
        for lag in range(1, lags):
            now += acc[lag][lag : lag + 1]
            later += acc[lag][lag - 1 : lag]
        nacc[g, 0:1, :] = now
        nacc[g, 1:2, :] = later

    agg_copy.wait()

    def solve(step, near, incoming):
        inc = incoming.astype(BF16)
        rows = [near[g] + mm(inc, agg_v[g], 1, 1)[g : g + 1] for g in range(gd)]
        sums[step, mine] = jnp.concatenate(rows, axis=0)

        def copy(peer, slot):
            return pltpu.make_async_remote_copy(
                src_ref=sums.at[step, mine],
                dst_ref=sums.at[step, slot],
                send_sem=sum_tx.at[step, peer],
                recv_sem=sum_rx.at[step, slot],
                device_id={"dir": peer},
                device_id_type=MESH,
            )

        for off in range(1, nd):
            copy(lax.rem(mine + off, nd), mine).start()
        for off in range(1, nd):
            peer = lax.rem(mine + off, nd)
            copy(peer, peer).wait_recv()
        total = sums[step, 0]
        for d in range(1, nd):
            total += sums[step, d]
        rest = exc_v[step] - total
        rest = jnp.concatenate([rest, rest], axis=0)
        high, low = parts(rest)
        both = jnp.concatenate([high, low], axis=0)
        rows = []
        for g in range(gd):
            a = mm(both, inv_hi[g], 1, 1)
            b = mm(high, inv_lo[g], 1, 1)
            rows.append(a[g : g + 1] + a[2 * gd + g : 2 * gd + g + 1] + b[g : g + 1])
        for off in range(1, nd):
            copy(lax.rem(mine + off, nd), mine).wait_send()
        stored = jnp.concatenate(rows, axis=0).astype(BF16)
        cur_o[step] = stored
        return stored

    def radiate(step, stored):
        twice = jnp.concatenate([stored.astype(F32)] * 2, axis=0).astype(BF16)
        rows = [mm(twice, agg_v[g])[g : g + 1] for g in range(gd)]
        spectrum = jnp.concatenate(rows, axis=0).astype(BF16)
        spec_o[step] = spectrum
        return spectrum

    p1_in()
    stored = solve(0, [nacc[g, 0:1, :] for g in range(gd)], unpack(jnp.sum(in1[...], axis=0)))
    wider = stored.astype(F32)
    for g in range(gd):
        cwin[gd + g] = wider[g : g + 1]
    cur_sides = send_sides(cwin, cwin_tx, cwin_rx)
    spectrum = radiate(0, stored).astype(F32)
    q = parts(jnp.concatenate([fresh * spectrum[s : s + 1] for s in range(gd)], axis=0))
    out2[...] = pack(older + mm(weight, q[0]) + mm(weight, q[1]))
    in2[me] = out2[me]
    p2_in, p2_out = send_all(lambda peer: out2.at[peer], in2, p2_tx, p2_rx)
    for c in cur_sides:
        c.wait_recv()
    near = []
    for g in range(gd):
        total = nacc[g, 1:2, :]
        for k in range(slots):
            local = jnp.clip(nbr_s[g, k] - (me - 1) * gd, 0, 3 * gd - 1)
            alive = (mine * slots + k < cnt_s[g]).astype(F32)
            row = (cwin[local] * alive).astype(BF16)
            total += mm(row, near_v[g, k, 0], 1, 1)
        near.append(total)
    p2_in()
    stored = solve(1, near, unpack(jnp.sum(in2[...], axis=0)))
    radiate(1, stored)
    for c in sides:
        c.wait_send()
    for c in cur_sides:
        c.wait_send()
    codes_out()
    p1_out()
    p2_out()


def per_device(
    currents_hist,
    spectra_hist,
    excitation,
    near_blocks,
    self_inverse,
    aggregate,
    translate,
    neighbours,
    counts,
    far_sources,
    far_classes,
    delays,
):
    n, nd = lax.axis_size("grp"), lax.axis_size("dir")
    gd, slots, lags, nb, _ = near_blocks.shape
    hf, _, dirs = spectra_hist.shape
    lane = dirs // 2 if dirs % 256 == 0 else dirs
    vmem = pl.BlockSpec(memory_space=pltpu.VMEM)
    anywhere = pl.BlockSpec(memory_space=pltpu.HBM)
    dma = pltpu.SemaphoreType.DMA
    return pl.pallas_call(
        functools.partial(kernel, n, nd),
        out_shape=(
            jax.ShapeDtypeStruct((STEPS, gd, nb), BF16),
            jax.ShapeDtypeStruct((STEPS, gd, dirs), BF16),
        ),
        in_specs=[anywhere] * 12,
        out_specs=(vmem, vmem),
        scratch_shapes=[
            pltpu.SMEM(neighbours.shape, jnp.int32),
            pltpu.SMEM(counts.shape, jnp.int32),
            pltpu.VMEM(currents_hist.shape, BF16),
            pltpu.VMEM(spectra_hist.shape, BF16),
            pltpu.VMEM(excitation.shape, F32),
            pltpu.VMEM(far_sources.shape, jnp.int32),
            pltpu.VMEM(far_classes.shape, jnp.int32),
            pltpu.VMEM((1,) + delays.shape, jnp.int32),
            pltpu.VMEM(translate.shape, F32),
            dma((9,)),
            pltpu.VMEM(near_blocks.shape, BF16),
            pltpu.VMEM(self_inverse.shape, F32),
            pltpu.VMEM(aggregate.shape, BF16),
            pltpu.VMEM(self_inverse.shape, BF16),
            pltpu.VMEM(self_inverse.shape, BF16),
            pltpu.VMEM((n, 2 * gd, 128), jnp.int32),
            pltpu.VMEM((3 * gd, 8, nb), F32),
            pltpu.VMEM((3 * gd, 1, nb), F32),
            pltpu.VMEM((gd, 8, nb), F32),
            pltpu.VMEM((n, 2 * gd, lane), F32),
            pltpu.VMEM((n, 2 * gd, lane), F32),
            pltpu.VMEM((n, 2 * gd, lane), F32),
            pltpu.VMEM((n, 2 * gd, lane), F32),
            pltpu.VMEM((STEPS, nd, gd, nb), F32),
            pltpu.VMEM((hf, gd, dirs), F32),
            dma((gd * slots,)),
            dma,
            dma,
            dma((n,)),
            dma((n,)),
            dma((2,)),
            dma((2,)),
            dma((2,)),
            dma((2,)),
            dma((n,)),
            dma((n,)),
            dma((n,)),
            dma((n,)),
            dma((STEPS, nd)),
            dma((STEPS, nd)),
        ],
        compiler_params=pltpu.CompilerParams(
            collective_id=0, has_side_effects=True, vmem_limit_bytes=62 * 1024 * 1024
        ),
        name="march",
    )(
        neighbours,
        counts,
        currents_hist,
        spectra_hist,
        excitation,
        far_sources,
        far_classes,
        delays.reshape(1, -1),
        translate,
        near_blocks,
        self_inverse,
        aggregate,
    )


def solution(mesh):
    placed = (
        P(None, "grp", None),
        P(None, "grp", "dir"),
        P(None, "grp", None),
        P("grp", "dir", None, None, None),
        P("grp", None, None),
        P("grp", None, "dir"),
        P(None, "dir"),
        P("grp", "dir"),
        P("grp"),
        P("grp", None),
        P("grp", None),
        P(),
    )
    return jax.shard_map(
        per_device,
        mesh=mesh,
        in_specs=placed,
        out_specs=(P(None, "grp", None), P(None, "grp", "dir")),
        check_vma=False,
    )
```
